32 devices in a mesh: dp: 4 (over x, core), ctx: 8 (over z, y).
Axes of the slice: x: 2, y: 2, z: 4, core: 2. Of those that a mesh axis runs over, the one named last changes fastest.
Arguments:
- queries: bfloat16 [4, 2048, 2048], P('dp', 'ctx'), may hold values from -19 to 19
- raw_keys: bfloat16 [4, 2048, 2048], P('dp', 'ctx'), may hold values from -6 to 6
- raw_values: bfloat16 [4, 2048, 2048], P('dp', 'ctx'), may hold values from -6 to 6
- beacon_queries: bfloat16 [4, 16, 2048], P('dp', 'ctx'), may hold values from -19 to 19
- beacon_keys: bfloat16 [4, 16, 2048], P('dp', 'ctx'), may hold values from -6 to 6
- beacon_values: bfloat16 [4, 16, 2048], P('dp', 'ctx'), may hold values from -6 to 6
- upstream: bfloat16 [4, 2048, 2048], P('dp', 'ctx'), may hold values from -6 to 6
- beacon_upstream: bfloat16 [4, 16, 2048], P('dp', 'ctx'), may hold values from -6 to 6
- key_gain: float32 [2048], replicated, may hold values from 0.1 to 1.9
- window: int32 [4], P('dp'), may hold values from 64 to 256, as said below
Outputs:
- grad_queries: bfloat16 [4, 2048, 2048], P('dp', 'ctx')
- grad_keys: bfloat16 [4, 2048, 2048], P('dp', 'ctx')
- grad_values: bfloat16 [4, 2048, 2048], P('dp', 'ctx')
- grad_beacon_queries: bfloat16 [4, 16, 2048], P('dp', 'ctx')
- grad_beacon_keys: bfloat16 [4, 16, 2048], P('dp', 'ctx')
- grad_beacon_values: bfloat16 [4, 16, 2048], P('dp', 'ctx')
- grad_gain: float32 [2048], replicated
The draws below stay inside these ranges and needn't reach their ends.
Inputs may be any that keep to these rules, and one draw needn't show every extreme that they name: One prompt's window is exactly 256 and one is exactly 64.
All inputs are finite; a program needn't handle non-finite values.
Results may differ from the reference program's by a relative error of at most 0.017.
Values may be sent and summed in bfloat16 or wider, within the bound.
No kernel may reach another device: no remote copies, remote signals or barrier semaphores. Data moves between devices by JAX's collectives and lax.ppermute only.
A program may use at most 192 MiB of HBM per device.

```python
import jax
import jax.numpy as jnp
from jax import lax

H = 16
DH = 128
INTERVAL = 128
S_DEV = 256
HD = 2048
PROMPTS = 4
L = 2048
NB = 16
N_CTX = 8


def beacon_draws(key):
    base = jax.random.fold_in(key, 31)
    key_query, key_key, key_beacon = jax.random.split(base, 3)
    queries = jax.random.truncated_normal(key_query, -6.0, 6.0, (PROMPTS, L, HD), jnp.float32)
    keys_raw = jax.random.truncated_normal(key_key, -6.0, 6.0, (PROMPTS, L, HD), jnp.float32)
    beacon_q = jax.random.truncated_normal(key_beacon, -6.0, 6.0, (PROMPTS, NB, HD), jnp.float32)
    return (queries.astype(jnp.bfloat16), keys_raw.astype(jnp.bfloat16), beacon_q.astype(jnp.bfloat16))


def draw_queries(key, part):
    return beacon_draws(key)[0]


def draw_raw_keys(key, part):
    return beacon_draws(key)[1]


def draw_beacon_queries(key, part):
    return beacon_draws(key)[2]


def draw_window(key, part):
    key_width, key_first, key_second = jax.random.split(jax.random.fold_in(key, 5), 3)
    widths = jax.random.randint(key_width, (PROMPTS,), S_DEV // 4, S_DEV + 1)
    first = jax.random.randint(key_first, (), 0, PROMPTS)
    second = (first + 1 + jax.random.randint(key_second, (), 0, PROMPTS - 1)) % PROMPTS
    widths = widths.at[second].set(S_DEV // 4).at[first].set(S_DEV)
    return widths.astype(jnp.int32)


def steps_of(rng, extent, shards, smallest, high):
    factor_of = 1.0
    for dim, shards_of in shards:
        draws = jax.random.uniform(jax.random.fold_in(jax.random.fold_in(rng, 6), dim), (shards_of,), jnp.float32, smallest / len(shards), high / len(shards))
        factor_of = factor_of * jnp.repeat(jnp.exp(draws), extent[dim] // shards_of).reshape((-1,) + (1,) * (len(extent) - 1 - dim))
    return factor_of


def centred(rng, dims, spread, limit, cuts=(), kind=jnp.bfloat16):
    result = spread * jax.random.normal(rng, dims, jnp.float32)
    if cuts:
        result = result * steps_of(rng, dims, cuts, -0.22, 0.18)
    return jnp.clip(result, -limit, limit).astype(kind)


def setup_inputs(seed: int = 0) -> dict:
    arg_keys = jax.random.split(jax.random.key(seed), 11)
    return {
        "queries": draw_queries(jax.random.fold_in(arg_keys[10], 71), 0),
        "raw_keys": draw_raw_keys(jax.random.fold_in(arg_keys[10], 71), 0),
        "raw_values": centred(arg_keys[2], (PROMPTS, L, HD), 1.0, 6.0, ((0, 4), (1, 8))),
        "beacon_queries": draw_beacon_queries(jax.random.fold_in(arg_keys[10], 71), 0),
        "beacon_keys": centred(arg_keys[4], (PROMPTS, NB, HD), 1.0, 6.0, ((0, 4), (1, 8))),
        "beacon_values": centred(arg_keys[5], (PROMPTS, NB, HD), 1.0, 6.0, ((0, 4), (1, 8))),
        "upstream": centred(arg_keys[6], (PROMPTS, L, HD), 1.0, 6.0, ((0, 4), (1, 8))),
        "beacon_upstream": centred(arg_keys[7], (PROMPTS, NB, HD), 1.0, 6.0, ((0, 4), (1, 8))),
        "key_gain": jnp.clip(1.0 + 0.18 * jax.random.normal(arg_keys[8], (HD,), jnp.float32), 0.1, 1.9),
        "window": draw_window(jax.random.fold_in(arg_keys[10], 71), 0),
    }


def slab_allowed(slab, width_here, slab_len, per_slab, beacon_count):
    position = slab * slab_len + jnp.arange(slab_len, dtype=jnp.int32)
    key_position = (slab - 1) * slab_len + jnp.arange(2 * slab_len, dtype=jnp.int32)
    column = jnp.arange(beacon_count, dtype=jnp.int32)
    own_beacon = slab * per_slab + jnp.arange(per_slab, dtype=jnp.int32)
    raw_raw = (key_position[None, :] <= position[:, None]) & (key_position[None, :] > position[:, None] - width_here) & (key_position[None, :] >= 0)
    raw_beacon = INTERVAL * (column[None, :] + 1) <= position[:, None] - width_here + 1
    beacon_raw = (key_position[None, :] >= INTERVAL * own_beacon[:, None]) & (key_position[None, :] < INTERVAL * (own_beacon[:, None] + 1))
    beacon_beacon = column[None, :] <= own_beacon[:, None]
    upper = jnp.concatenate([raw_raw, raw_beacon], axis=1)
    lower = jnp.concatenate([beacon_raw, beacon_beacon], axis=1)
    return jnp.concatenate([upper, lower], axis=0)


def attend(query_block, grad_block, key_block, value_block, allowed):
    scale = DH ** -0.5
    query_f = query_block.astype(jnp.float32).reshape(query_block.shape[0], H, DH)
    grad_f = grad_block.astype(jnp.float32).reshape(grad_block.shape[0], H, DH)
    key_f = key_block.astype(jnp.float32).reshape(key_block.shape[0], H, DH)
    value_f = value_block.astype(jnp.float32).reshape(value_block.shape[0], H, DH)
    scores = jnp.einsum('rhd,khd->hrk', query_f, key_f) * scale
    scores = jnp.where(allowed[None], scores, -jnp.inf)
    peak = jnp.max(scores, axis=-1, keepdims=True)
    expo = jnp.exp(scores - peak)
    total = jnp.sum(expo, axis=-1, keepdims=True)
    probs = expo / total
    probs_low = lax.optimization_barrier(probs.astype(jnp.bfloat16)).astype(jnp.float32)
    output = jnp.einsum('hrk,khd->rhd', probs_low, value_f)
    delta = jnp.sum(grad_f * output, axis=-1).T[:, :, None]
    dprob = jnp.einsum('rhd,khd->hrk', grad_f, value_f)
    dscore = probs * (dprob - delta)
    dscore_low = lax.optimization_barrier(dscore.astype(jnp.bfloat16)).astype(jnp.float32)
    dquery = jnp.einsum('hrk,khd->rhd', dscore_low, key_f) * scale
    dkey = jnp.einsum('hrk,rhd->khd', dscore_low, query_f) * scale
    dvalue = jnp.einsum('hrk,rhd->khd', probs_low, grad_f)
    return dquery.reshape(query_block.shape[0], HD), dkey.reshape(key_block.shape[0], HD), dvalue.reshape(key_block.shape[0], HD)


def reference(queries, raw_keys, raw_values, beacon_queries, beacon_keys, beacon_values, upstream, beacon_upstream, key_gain, window):
    per_slab = S_DEV // INTERVAL

    def one_prompt(packed):
        q_p, k_p, v_p, bq_p, bk_p, bv_p, g_p, bg_p, width_here = packed
        gained = (bk_p.astype(jnp.float32) * key_gain).astype(jnp.bfloat16)

        def one_slab(slab):
            start = slab * S_DEV
            prev_start = jnp.maximum(start - S_DEV, 0).astype(jnp.int32)
            bstart = (slab * per_slab).astype(jnp.int32)
            query_block = jnp.concatenate([lax.dynamic_slice_in_dim(q_p, start, S_DEV, 0), lax.dynamic_slice_in_dim(bq_p, bstart, per_slab, 0)], axis=0)
            grad_block = jnp.concatenate([lax.dynamic_slice_in_dim(g_p, start, S_DEV, 0), lax.dynamic_slice_in_dim(bg_p, bstart, per_slab, 0)], axis=0)
            key_block = jnp.concatenate([lax.dynamic_slice_in_dim(k_p, prev_start, S_DEV, 0), lax.dynamic_slice_in_dim(k_p, start, S_DEV, 0), gained], axis=0)
            value_block = jnp.concatenate([lax.dynamic_slice_in_dim(v_p, prev_start, S_DEV, 0), lax.dynamic_slice_in_dim(v_p, start, S_DEV, 0), bv_p], axis=0)
            allowed = slab_allowed(slab, width_here, S_DEV, per_slab, NB)
            return attend(query_block, grad_block, key_block, value_block, allowed)

        dq_all, dk_all, dv_all = lax.map(one_slab, jnp.arange(N_CTX, dtype=jnp.int32))
        pad = jnp.zeros((1, S_DEV, HD), jnp.float32)
        dq_raw = dq_all[:, :S_DEV].reshape(L, HD)
        dq_beacon = dq_all[:, S_DEV:].reshape(NB, HD)
        dk_raw = (dk_all[:, S_DEV:2 * S_DEV] + jnp.concatenate([dk_all[1:, :S_DEV], pad], axis=0)).reshape(L, HD)
        dv_raw = (dv_all[:, S_DEV:2 * S_DEV] + jnp.concatenate([dv_all[1:, :S_DEV], pad], axis=0)).reshape(L, HD)
        gained_grad = jnp.sum(dk_all[:, 2 * S_DEV:], axis=0)
        beacon_value_grad = jnp.sum(dv_all[:, 2 * S_DEV:], axis=0)
        gain_term = jnp.sum(bk_p.astype(jnp.float32) * gained_grad, axis=0)
        return (dq_raw.astype(jnp.bfloat16), dk_raw.astype(jnp.bfloat16), dv_raw.astype(jnp.bfloat16),
                dq_beacon.astype(jnp.bfloat16), (key_gain * gained_grad).astype(jnp.bfloat16),
                beacon_value_grad.astype(jnp.bfloat16), gain_term)

    results = lax.map(one_prompt, (queries, raw_keys, raw_values, beacon_queries, beacon_keys, beacon_values, upstream, beacon_upstream, window))
    return (results[0], results[1], results[2], results[3], results[4], results[5], jnp.sum(results[6], axis=0))
```

```python
from functools import partial

import jax
import jax.numpy as jnp
from jax import lax
from jax.experimental import pallas as pl
from jax.experimental.pallas import tpu as pltpu
from jax.sharding import PartitionSpec as P

DH = 128
INTERVAL = 128
SCALE = DH ** (-0.5)
GROUP = 8
MASKED = -1e30
VMEM_LIMIT = 48 * 1024 * 1024


def passed_along(block, axis, distance):
    devices = range(lax.axis_size(axis))
    route = [(i - distance, i) for i in devices if i - distance in devices]
    return lax.ppermute(block, axis, route)


def dot_nt(a, b):
    return lax.dot_general(a, b, (((1,), (1,)), ((), ())), preferred_element_type=jnp.float32)


def dot_nn(a, b):
    return lax.dot_general(a, b, (((1,), (0,)), ((), ())), preferred_element_type=jnp.float32)


def dot_tn(a, b):
    return lax.dot_general(a, b, (((0,), (0,)), ((), ())), preferred_element_type=jnp.float32)


def iotas(shape):
    return lax.broadcasted_iota(jnp.int32, shape, 0), lax.broadcasted_iota(jnp.int32, shape, 1)


def own_mask(count, width):
    col, row = iotas((count, count))
    return (col <= row) & (col > row - width)


def beacon_mask(beacons, rows, first_row, width):
    col, row = iotas((beacons, rows))
    return INTERVAL * (col + 1) <= first_row + row - width + 1


def own_stats_kernel(info_ref, q_ref, k_ref, v_ref, g_ref, stats_ref):
    width = info_ref[0]
    count = q_ref.shape[0]
    mask = own_mask(count, width)
    for h in range(GROUP):
        at = slice(h * DH, (h + 1) * DH)
        s = jnp.where(mask, dot_nt(k_ref[:, at], q_ref[:, at]), MASKED)
        dp = dot_nt(v_ref[:, at], g_ref[:, at])
        m = jnp.max(s, axis=0, keepdims=True)
        e = jnp.exp((s - m) * SCALE)
        stats_ref[0, 0, h : h + 1, :] = m
        stats_ref[0, 1, h : h + 1, :] = jnp.sum(e, axis=0, keepdims=True)
        stats_ref[0, 2, h : h + 1, :] = jnp.sum(e * dp, axis=0, keepdims=True)


def cross_kernel(
    info_ref, q_ref, g_ref, k_ref, v_ref, bk_ref, bv_ref, st_ref, dq_ref, dk_ref, dv_ref, out_ref
):
    width, slab, absent = info_ref[0], info_ref[1], info_ref[2]
    count, beacons = k_ref.shape[0], bk_ref.shape[0]
    col, row = iotas((count, count))
    mask = (col - row > count - width) & (absent == 0)
    mask_b = beacon_mask(beacons, count, (slab + 1) * count, width)
    spare = absent.astype(jnp.float32)
    for h in range(GROUP):
        at = slice(h * DH, (h + 1) * DH)
        q, g, k, v = q_ref[:, at], g_ref[:, at], k_ref[:, at], v_ref[:, at]
        m1, z1, d1 = (st_ref[0, i, h : h + 1, :] for i in range(3))
        s = jnp.where(mask, dot_nt(k, q), MASKED)
        dp = dot_nt(v, g)
        sb = jnp.where(mask_b, dot_nt(bk_ref[:, at], q), MASKED)
        dpb = dot_nt(bv_ref[:, at], g)
        m = jnp.maximum(jnp.max(s, axis=0, keepdims=True), jnp.max(sb, axis=0, keepdims=True))
        m = jnp.maximum(m, m1)
        e = jnp.exp((s - m) * SCALE)
        eb = jnp.exp((sb - m) * SCALE)
        a1 = jnp.exp((m1 - m) * SCALE)
        z2 = jnp.sum(e, axis=0, keepdims=True)
        d2 = jnp.sum(e * dp, axis=0, keepdims=True)
        z = z1 * a1 + z2 + jnp.sum(eb, axis=0, keepdims=True) + spare
        d = d1 * a1 + d2 + jnp.sum(eb * dpb, axis=0, keepdims=True)
        zi = 1.0 / z
        p = e * zi
        ds = (p * (dp - d * zi)).astype(jnp.bfloat16)
        dv_ref[:, at] = dot_nn(p.astype(jnp.bfloat16), g)
        dk_ref[:, at] = dot_nn(ds, q)
        dq_ref[:, at] = (dot_tn(ds, k) * SCALE).astype(jnp.bfloat16)
        out_ref[0, 0, h : h + 1, :] = m
        out_ref[0, 1, h : h + 1, :] = z2
        out_ref[0, 2, h : h + 1, :] = d2


def own_kernel(
    info_ref, q_ref, g_ref, k_ref, v_ref, bk_ref, bv_ref, st_ref, dk2_ref, dv2_ref, bq_ref, bg_ref,
    ak_ref, dq_ref, dk_ref, dv_ref, dqb_ref, part_ref, gain_ref,
):
    width, slab = info_ref[0], info_ref[1]
    count, beacons = k_ref.shape[0], bk_ref.shape[0]
    lanes = bq_ref.shape[0]
    per_slab = lanes // GROUP
    mask = jnp.concatenate(
        [own_mask(count, width), beacon_mask(beacons, count, slab * count, width)], axis=0
    )
    first = slab == 0

    col, lane = iotas((count, lanes))
    own = lane % per_slab
    mask_raw = (col >= INTERVAL * own) & (col < INTERVAL * (own + 1))
    col, lane = iotas((beacons, lanes))
    mask_b = col <= slab * per_slab + lane % per_slab
    kc = jnp.concatenate([k_ref[...], bk_ref[...]], axis=0)
    vc = jnp.concatenate([v_ref[...], bv_ref[...]], axis=0)
    bq, bg = bq_ref[...], bg_ref[...]
    s = jnp.where(jnp.concatenate([mask_raw, mask_b], axis=0), dot_nt(kc, bq), MASKED)
    dp = dot_nt(vc, bg)
    m = jnp.max(s, axis=0, keepdims=True)
    e = jnp.exp((s - m) * SCALE)
    zi = 1.0 / jnp.sum(e, axis=0, keepdims=True)
    p = e * zi
    ds = (p * (dp - jnp.sum(p * dp, axis=0, keepdims=True))).astype(jnp.bfloat16)
    dvb = dot_nn(p.astype(jnp.bfloat16), bg)
    dkb = dot_nn(ds, bq)
    row, column = iotas((lanes, GROUP * DH))
    dqb_ref[0] = jnp.where(row // per_slab == column // DH, dot_tn(ds, kc) * SCALE, 0.0)

    for h in range(GROUP):
        at = slice(h * DH, (h + 1) * DH)
        q, g = q_ref[:, at], g_ref[:, at]
        k, v = kc[:, at], vc[:, at]
        m2, z2, d2 = (st_ref[0, i, h : h + 1, :] for i in range(3))
        m2 = jnp.where(first, MASKED, m2)
        s = jnp.where(mask, dot_nt(k, q), MASKED)
        dp = dot_nt(v, g)
        m = jnp.maximum(jnp.max(s, axis=0, keepdims=True), m2)
        e = jnp.exp((s - m) * SCALE)
        a2 = jnp.exp((m2 - m) * SCALE)
        z = jnp.sum(e, axis=0, keepdims=True) + z2 * a2
        d = jnp.sum(e * dp, axis=0, keepdims=True) + d2 * a2
        zi = 1.0 / z
        p = e * zi
        ds = (p * (dp - d * zi)).astype(jnp.bfloat16)
        dv = dot_nn(p.astype(jnp.bfloat16), g) + dvb[:, at]
        dk = (dot_nn(ds, q) + dkb[:, at]) * SCALE
        dq_ref[:, at] = dot_tn(ds, k) * SCALE
        dk_ref[:, at] = (dk[:count] + dk2_ref[:, at] * SCALE).astype(jnp.bfloat16)
        dv_ref[:, at] = (dv[:count] + dv2_ref[:, at]).astype(jnp.bfloat16)
        part_ref[0, :, at] = dk[count:].astype(jnp.bfloat16)
        part_ref[1, :, at] = dv[count:].astype(jnp.bfloat16)
        gain = jnp.sum(ak_ref[:, at].astype(jnp.float32) * dk[count:], axis=0, keepdims=True)
        gain_ref[:, at] = jnp.broadcast_to(gain, (8, DH))


def on_device(
    queries,
    raw_keys,
    raw_values,
    beacon_queries,
    beacon_keys,
    beacon_values,
    upstream,
    beacon_upstream,
    key_gain,
    window,
):
    _, count, width_all = queries.shape
    per_slab = beacon_queries.shape[1]
    slabs = lax.axis_size("ctx")
    slab = lax.axis_index("ctx")
    beacons = per_slab * slabs
    heads = width_all // DH
    groups = heads // GROUP
    lanes = GROUP * per_slab
    wide = GROUP * DH
    q, k, v, g = queries[0], raw_keys[0], raw_values[0], upstream[0]
    info = jnp.stack([window[0], slab.astype(jnp.int32), (slab == slabs - 1).astype(jnp.int32)])

    smem = pl.BlockSpec(memory_space=pltpu.SMEM)
    rows_spec = pl.BlockSpec((count, wide), lambda i: (0, i))
    beacon_spec = pl.BlockSpec((beacons, wide), lambda i: (0, i))
    stats_spec = pl.BlockSpec((1, 3, GROUP, count), lambda i: (i, 0, 0, 0))
    diag_spec = pl.BlockSpec((lanes, wide), lambda i: (i, i))
    params = pltpu.CompilerParams(vmem_limit_bytes=VMEM_LIMIT)
    f32, bf16 = jnp.float32, jnp.bfloat16
    rows_f32 = jax.ShapeDtypeStruct((count, width_all), f32)
    rows_bf16 = jax.ShapeDtypeStruct((count, width_all), bf16)
    stats_shape = jax.ShapeDtypeStruct((groups, 3, GROUP, count), f32)

    def cost(matmuls):
        work = 2 * count * count * width_all
        return pl.CostEstimate(
            flops=matmuls * work, bytes_accessed=8 * count * width_all, transcendentals=heads * count * count
        )

    next_q, next_g = passed_along(q, "ctx", -1), passed_along(g, "ctx", -1)
    own_stats = pl.pallas_call(
        own_stats_kernel,
        grid=(groups,),
        in_specs=[smem, rows_spec, rows_spec, rows_spec, rows_spec],
        out_specs=stats_spec,
        out_shape=stats_shape,
        compiler_params=params,
        cost_estimate=cost(2),
        name="own_stats",
    )(info, q, k, v, g)
    next_stats = passed_along(own_stats, "ctx", -1)

    beacon_pair = jnp.concatenate([beacon_keys, beacon_values], axis=1)
    beacon_pair, _ = lax.optimization_barrier((beacon_pair, own_stats))
    gathered = lax.all_to_all(
        jnp.broadcast_to(beacon_pair, (slabs, 2 * per_slab, width_all)), "ctx", 0, 0, tiled=True
    )
    all_keys = gathered[:, :per_slab].reshape(beacons, width_all)
    all_values = gathered[:, per_slab:].reshape(beacons, width_all)
    gained = (all_keys.astype(f32) * key_gain).astype(bf16)

    dq_next, dk_cross, dv_cross, cross_stats = pl.pallas_call(
        cross_kernel,
        grid=(groups,),
        in_specs=[smem] + [rows_spec] * 4 + [beacon_spec] * 2 + [stats_spec],
        out_specs=[rows_spec, rows_spec, rows_spec, stats_spec],
        out_shape=[rows_bf16, rows_f32, rows_f32, stats_shape],
        compiler_params=params,
        cost_estimate=cost(5),
        name="cross",
    )(info, next_q, next_g, k, v, gained, all_values, next_stats)
    prev_stats = passed_along(cross_stats, "ctx", 1)
    prev_dq = passed_along(dq_next, "ctx", 1)

    head_of_row = jnp.arange(heads * per_slab, dtype=jnp.int32)[:, None] // per_slab
    head_of_column = jnp.arange(width_all, dtype=jnp.int32)[None, :] // DH
    same_head = head_of_row == head_of_column

    def per_head(block):
        return jnp.where(same_head, jnp.tile(block, (heads, 1)), 0).astype(bf16)

    dq_own, dk, dv, dq_beacon, part, gain = pl.pallas_call(
        own_kernel,
        grid=(groups,),
        in_specs=[smem] + [rows_spec] * 4 + [beacon_spec] * 2 + [stats_spec] + [rows_spec] * 2
        + [diag_spec] * 2 + [beacon_spec],
        out_specs=[
            rows_spec, rows_spec, rows_spec,
            pl.BlockSpec((1, lanes, wide), lambda i: (i, 0, 0)),
            pl.BlockSpec((2, beacons, wide), lambda i: (0, 0, i)),
            pl.BlockSpec((8, wide), lambda i: (0, i)),
        ],
        out_shape=[
            rows_f32, rows_bf16, rows_bf16,
            jax.ShapeDtypeStruct((groups, lanes, wide), f32),
            jax.ShapeDtypeStruct((2, beacons, width_all), bf16),
            jax.ShapeDtypeStruct((8, width_all), f32),
        ],
        compiler_params=params,
        cost_estimate=cost(5),
        name="own",
    )(
        info, q, g, k, v, gained, all_values, prev_stats, dk_cross, dv_cross,
        per_head(beacon_queries[0]), per_head(beacon_upstream[0]), all_keys,
    )
    grad_queries = (dq_own + prev_dq.astype(f32)).astype(bf16)
    grad_beacon_queries = jnp.sum(dq_beacon.reshape(groups, GROUP, per_slab, wide), axis=1)
    grad_beacon_queries = grad_beacon_queries.transpose(1, 0, 2).reshape(per_slab, width_all)

    part = part.reshape(2, slabs, per_slab, width_all).transpose(1, 0, 2, 3)
    terms = lax.all_to_all(part, "ctx", 0, 0, tiled=True)
    own_terms = jnp.sum(terms.astype(f32), axis=0)
    grad_gain = lax.all_to_all(
        jnp.broadcast_to(gain[:1], (lax.axis_size("dp") * slabs, width_all)), ("dp", "ctx"), 0, 0, tiled=True
    )
    grad_gain = jnp.sum(grad_gain, axis=0)
    return (
        grad_queries[None],
        dk[None],
        dv[None],
        grad_beacon_queries.astype(bf16)[None],
        (key_gain * own_terms[0]).astype(bf16)[None],
        own_terms[1].astype(bf16)[None],
        grad_gain,
    )


def solution(mesh):
    split = P("dp", "ctx", None)
    in_specs = (split,) * 8 + (P(), P("dp"))
    out_specs = (split,) * 6 + (P(),)
    return jax.shard_map(
        on_device, mesh=mesh, in_specs=in_specs, out_specs=out_specs, check_vma=False
    )
```
